256 devices in a mesh: row: 8 (over z), col: 32 (over y, x, core).
Axes of the slice: x: 4, y: 4, z: 8, core: 2. Of those that a mesh axis runs over, the one named last changes fastest.
Arguments:
- activations: bfloat16 [8192, 6144], P('col', 'row'), may hold values from -30 to 30
- out_grads: bfloat16 [8192, 24576], P('row', 'col'), may hold values from -0.3 to 0.3
- projector: bfloat16 [6144, 512], P('row'), may hold values from -0.078125 to 0.078125
- first_moment: float32 [512, 24576], P(None, 'col'), may hold values from -6 to 6
- second_moment: float32 [512, 24576], P(None, 'col'), may hold values from 0.05 to 2
- prev_norm: float32 [1], replicated, may hold values from 0.3 to 1
Outputs:
- step_update: float32 [6144, 24576], P('row', 'col')
- new_first: float32 [512, 24576], P(None, 'col')
- new_second: float32 [512, 24576], P(None, 'col')
The draws below stay inside these ranges and needn't reach their ends.
All inputs are finite; a program needn't handle non-finite values.
Results may differ from the reference program's by a relative error of at most 0.0003.
Values may be sent and summed in bfloat16 or wider, within the bound.
No kernel may reach another device: no remote copies, remote signals or barrier semaphores. Data moves between devices by JAX's collectives and lax.ppermute only.
A program may use at most 128 MiB of HBM per device.

```python
import math
import jax
import jax.numpy as jnp
from jax import lax

D = 6144
FF = 24576
RANK = 512
TOKENS = 8192


def draw_activations(key, part):
    key = jax.random.fold_in(key, 11)
    raw_key, scale_key = jax.random.split(key, 2)
    feature_scale = 10.0 ** jax.random.uniform(scale_key, (D,)) * 3.0 ** (jnp.arange(D, dtype=jnp.float32) / D) / 5.0
    raw_values = jax.random.normal(raw_key, (TOKENS, D))
    return (jnp.clip(raw_values, -5.0, 5.0) * feature_scale[None, :]).astype(jnp.bfloat16)


def draw_out_grads(key, part):
    key = jax.random.fold_in(key, 23)
    raw_key, row_key, col_key = jax.random.split(key, 3)
    token_scale = 10.0 ** jax.random.uniform(row_key, (TOKENS,))
    unit_scale = 10.0 ** jax.random.uniform(col_key, (FF,)) * 3.0 ** (jnp.arange(FF, dtype=jnp.float32) / FF)
    raw_values = jax.random.normal(raw_key, (TOKENS, FF))
    return (jnp.clip(raw_values, -5.0, 5.0) * token_scale[:, None] * unit_scale[None, :] / 5000.0).astype(jnp.bfloat16)


def shard_levels(stream_key, extent, shards, smallest, largest):
    gain = 1.0
    for position, shards_of in shards:
        draws = jax.random.uniform(jax.random.fold_in(jax.random.fold_in(stream_key, 6), position), (shards_of,), jnp.float32, smallest / len(shards), largest / len(shards))
        gain = gain * jnp.repeat(jnp.exp(draws), extent[position] // shards_of).reshape((-1,) + (1,) * (len(extent) - 1 - position))
    return gain


def centred(stream_key, extent, width, reach, shards=(), held_as=jnp.bfloat16):
    entries = jax.random.normal(stream_key, extent, jnp.float32) * width
    if len(shards) > 0:
        entries = shard_levels(stream_key, extent, shards, -0.22, 0.18) * entries
    return jnp.clip(entries, min=-reach, max=reach).astype(held_as)


def setup_inputs(seed: int = 0) -> dict:
    splits = jax.random.split(jax.random.key(seed), 7)
    activations = draw_activations(jax.random.fold_in(splits[6], 71), 0)
    out_grads = draw_out_grads(jax.random.fold_in(splits[6], 71), 0)
    projector = centred(splits[2], (D, RANK), D ** -0.5, 0.078125, ((0, 8),))
    first_moment = centred(splits[3], (RANK, FF), 1.0, 6.0, ((1, 32),), jnp.float32)
    second_moment = jnp.clip(jnp.exp(math.log(2.0) - 3.6888794 * jax.random.uniform(splits[4], (RANK, FF), jnp.float32) ** shard_levels(splits[4], (RANK, FF), ((1, 32),), -0.2, 0.2)), 0.05, 2.0)
    prev_norm = jnp.clip(jax.random.uniform(splits[5], (1,), jnp.float32, 0.3, 1.0), 0.3, 1.0)
    return {"activations": activations, "out_grads": out_grads, "projector": projector, "first_moment": first_moment, "second_moment": second_moment, "prev_norm": prev_norm}


beta_one = 0.9
beta_two = 0.95
corr_one = 1.0 - 0.9 ** 10
corr_two = 1.0 - 0.95 ** 10
growth = 1.01

def reference(activations, out_grads, projector, first_moment, second_moment, prev_norm):
    weight_grad = jnp.dot(activations.T, out_grads, preferred_element_type=jnp.float32)
    proj_wide = projector.astype(jnp.float32)
    projected = jnp.dot(proj_wide.T, weight_grad, precision=lax.Precision.HIGHEST)
    residual = weight_grad - jnp.dot(proj_wide, projected, precision=lax.Precision.HIGHEST)
    resid_sq = lax.optimization_barrier(jnp.sum(residual * residual, axis=0))
    new_first = beta_one * first_moment + (1.0 - beta_one) * projected
    new_second = beta_two * second_moment + (1.0 - beta_two) * projected * projected
    adam_dir = new_first / corr_one / (jnp.sqrt(new_second / corr_two) + 1e-08)
    col_scale = jnp.sqrt(lax.optimization_barrier(jnp.sum(adam_dir * adam_dir, axis=0))) / jnp.sqrt(lax.optimization_barrier(jnp.sum(projected * projected, axis=0)) + 1e-06)
    total_norm = jnp.sqrt(jnp.sum(col_scale * col_scale * resid_sq) / (D * FF) + 1e-06)
    clip_factor = growth * prev_norm[0] / total_norm
    low_rank = jnp.dot(proj_wide, adam_dir, precision=lax.Precision.HIGHEST)
    step_update = low_rank + (clip_factor * col_scale)[None, :] * residual
    return (step_update, new_first, new_second)
```

```python
import functools

import jax
import jax.numpy as jnp
from jax import lax
from jax.experimental import pallas as pl
from jax.experimental.pallas import tpu as pltpu
from jax.sharding import PartitionSpec as P

D = 6144
FF = 24576
RANK = 512

beta_one = 0.9
beta_two = 0.95
corr_one = 1.0 - 0.9**10
corr_two = 1.0 - 0.95**10
growth = 1.01

ROWS = 8
COLS = 32
DR = D // ROWS
FC = FF // COLS
TK = 256
TS = 4
CB = 256
CW = 256
RB = RANK // ROWS
SB = TS * TK // CB
VMEM_LIMIT = 24 * 1024 * 1024
VMEM_MOST = 58 * 1024 * 1024
STEP_FLOPS = 8.0e9


def whole(shape):
    return pl.BlockSpec(shape, lambda *_: (0,) * len(shape))


def prologue_kernel(act_ref, proj_ref, at_ref, yt_ref):
    at = act_ref[...].T
    at_ref[...] = at
    yt_ref[...] = lax.dot_general(
        proj_ref[...], at, (((0,), (0,)), ((), ())), preferred_element_type=jnp.float32
    )


def prologue(activations, projector):
    return pl.pallas_call(
        prologue_kernel,
        out_shape=[
            jax.ShapeDtypeStruct((DR, CB), jnp.bfloat16),
            jax.ShapeDtypeStruct((RANK, CB), jnp.float32),
        ],
        compiler_params=pltpu.CompilerParams(vmem_limit_bytes=VMEM_LIMIT),
    )(activations, projector)


def product_kernel(count, ranked, resumed, waited, ids, *refs):
    refs = list(refs)
    lefts = [refs.pop(0) for _ in ranked]
    starts = [refs.pop(0) for _ in ranked] if resumed else None
    pieces, refs = refs[: TS * count], refs[TS * count + waited :]
    outs, held, (right_held, sems, right_sems) = refs[: len(ranked)], refs[len(ranked) : -3], refs[-3:]

    def right_copy(index, t):
        return pltpu.make_async_copy(
            pieces[TS * index + t], right_held.at[index, pl.ds(t * TK, TK)], right_sems.at[index, t]
        )

    def copy(which, index):
        rows = pl.ds(ids[index] * SB, SB)
        return pltpu.make_async_copy(lefts[which].at[rows], held[which].at[index], sems.at[which, index])

    for index in range(count):
        for t in range(TS):
            right_copy(index, t).start()
        for which in range(len(ranked)):
            copy(which, index).start()
    for index in range(count):
        for t in range(TS):
            right_copy(index, t).wait()
        right = right_held[index]
        for which, is_ranked in enumerate(ranked):
            copy(which, index).wait()
            left = held[which]
            wide = jnp.concatenate([left[index, block] for block in range(SB)], axis=1)
            got = jnp.dot(wide, right, preferred_element_type=jnp.float32)
            part = got[:RB] + got[RB:] if is_ranked else got
            out = outs[which]
            if index > 0:
                out[...] += part
            else:
                out[...] = starts[which][...] + part if resumed else part


def products(ids, pieces, lefts, ranked, starts=(), waited=()):
    count = len(pieces) // TS
    resumed = len(starts) > 0
    width = pieces[0].shape[1]
    specs = [pl.BlockSpec(memory_space=pltpu.SMEM)]
    specs += [pl.BlockSpec(memory_space=pltpu.HBM)] * len(lefts)
    specs += [pl.BlockSpec(memory_space=pltpu.VMEM)] * len(starts)
    specs += [pl.BlockSpec(memory_space=pltpu.HBM)] * (len(pieces) + len(waited))
    heights, rows = [], 0
    for left, is_ranked in zip(lefts, ranked):
        rows += left.shape[1]
        heights.append(RB if is_ranked else left.shape[1])
    return pl.pallas_call(
        functools.partial(product_kernel, count, ranked, resumed, len(waited)),
        out_shape=[jax.ShapeDtypeStruct((h, width), jnp.float32) for h in heights],
        in_specs=specs,
        out_specs=[pl.BlockSpec(memory_space=pltpu.VMEM)] * len(heights),
        scratch_shapes=[
            *[pltpu.VMEM((count, SB) + left.shape[1:], jnp.bfloat16) for left in lefts],
            pltpu.VMEM((count, TS * TK, width), jnp.bfloat16),
            pltpu.SemaphoreType.DMA((len(lefts), count)),
            pltpu.SemaphoreType.DMA((count, TS)),
        ],
        compiler_params=pltpu.CompilerParams(vmem_limit_bytes=VMEM_MOST),
        cost_estimate=pl.CostEstimate(
            flops=2 * rows * TS * TK * width * count,
            bytes_accessed=count * TS * TK * (rows + width) * 2 + rows * width * 4,
            transcendentals=0,
        ),
    )(ids, *lefts, *starts, *pieces, *waited)


def halves(values):
    high = values.astype(jnp.bfloat16)
    return high, (values - high.astype(jnp.float32)).astype(jnp.bfloat16)


def times(left, values):
    high, low = halves(values)
    return jnp.dot(left, high, preferred_element_type=jnp.float32) + jnp.dot(
        left, low, preferred_element_type=jnp.float32
    )


def column_kernel(where, w_ref, *refs):
    refs = list(refs)
    pieces = [refs.pop(0) for _ in range(ROWS + 1)]
    proj_ref, m1_ref, m2_ref, scaled_ref, low_ref, n1_ref, n2_ref, sum_out, projected_ref = refs
    me = where[0]
    for piece, hop in zip(pieces, (0, 1, 2, 3, -1, -2, -3)):
        block = lax.rem(me - hop + ROWS, ROWS)
        projected_ref[pl.ds(pl.multiple_of(block * RB, RB), RB), :] = piece[...]
    block = lax.rem(me + 4, ROWS)
    opposite = jnp.concatenate([pieces[-2][...], pieces[-1][...]], axis=0)
    projected_ref[pl.ds(pl.multiple_of(block * RB, RB), RB), :] = opposite
    projected = projected_ref[...]
    new_first = beta_one * m1_ref[...] + (1.0 - beta_one) * projected
    square = projected * projected
    new_second = beta_two * m2_ref[...] + (1.0 - beta_two) * square
    n1_ref[...] = new_first
    n2_ref[...] = new_second
    adam_dir = new_first * (1.0 / corr_one) / (jnp.sqrt(new_second * (1.0 / corr_two)) + 1e-08)
    col_scale = jnp.sqrt(jnp.sum(adam_dir * adam_dir, axis=0, keepdims=True)) / jnp.sqrt(
        jnp.sum(square, axis=0, keepdims=True) + 1e-06
    )
    left = proj_ref[...]
    residual = w_ref[...] - times(left, projected)
    resid_sq = jnp.sum(residual * residual, axis=0, keepdims=True)
    scaled_ref[...] = col_scale * residual
    low_ref[...] = times(left, adam_dir)
    total = jnp.sum(col_scale * col_scale * resid_sq, axis=1, keepdims=True)
    total = jnp.broadcast_to(total[None], sum_out.shape)

    @pl.when(pl.program_id(0) == 0)
    def _():
        sum_out[...] = total

    @pl.when(pl.program_id(0) > 0)
    def _():
        sum_out[...] += total


def columns(where, w, pieces, projector, first, second):
    def block(rows):
        return pl.BlockSpec((rows, CW), lambda i, ids: (0, i))

    args = [w, *pieces, projector, first, second]
    specs = [block(w.shape[0])] + [block(x.shape[0]) for x in pieces]
    specs += [whole(projector.shape), block(RANK), block(RANK)]
    return pl.pallas_call(
        column_kernel,
        out_shape=[
            jax.ShapeDtypeStruct((DR, FC), jnp.float32),
            jax.ShapeDtypeStruct((DR, FC), jnp.float32),
            jax.ShapeDtypeStruct((RANK, FC), jnp.float32),
            jax.ShapeDtypeStruct((RANK, FC), jnp.float32),
            jax.ShapeDtypeStruct((ROWS, 8, 128), jnp.float32),
        ],
        grid_spec=pltpu.PrefetchScalarGridSpec(
            num_scalar_prefetch=1,
            grid=(FC // CW,),
            in_specs=specs,
            out_specs=[block(DR), block(DR), block(RANK), block(RANK), whole((ROWS, 8, 128))],
            scratch_shapes=[pltpu.VMEM((RANK, CW), jnp.float32)],
        ),
        compiler_params=pltpu.CompilerParams(vmem_limit_bytes=VMEM_LIMIT),
        cost_estimate=pl.CostEstimate(
            flops=8 * DR * RANK * FC, bytes_accessed=16 * RANK * FC + 12 * DR * FC, transcendentals=0
        ),
    )(where, *args)


def final_kernel(prev_ref, sums_ref, scaled_ref, low_ref, out_ref):
    total = jnp.sum(sums_ref[...], axis=0)[:1, :1]
    clip = growth * prev_ref[0] / jnp.sqrt(total / (D * FF) + 1e-06)
    out_ref[...] = low_ref[...] + clip * scaled_ref[...]


def final(prev_norm, sums, scaled, low):
    tile = pl.BlockSpec((128, FC), lambda i: (i, 0))
    return pl.pallas_call(
        final_kernel,
        out_shape=jax.ShapeDtypeStruct((DR, FC), jnp.float32),
        grid=(DR // 128,),
        in_specs=[pl.BlockSpec(memory_space=pltpu.SMEM), whole(sums.shape), tile, tile],
        out_specs=tile,
        compiler_params=pltpu.CompilerParams(vmem_limit_bytes=VMEM_LIMIT),
    )(prev_norm, sums, scaled, low)


def shift(values, by):
    return lax.ppermute(values, "row", [(i, (i + by) % ROWS) for i in range(ROWS)])


def gated(values, after):
    values, *after = lax.optimization_barrier((values, *after))
    return values, after


def mark_kernel(mark_ref, out_ref):
    out_ref[...] = mark_ref[...]


def step_mark(mark, waited):
    mark, waited = gated(mark, waited)
    mark = pl.pallas_call(
        mark_kernel,
        out_shape=jax.ShapeDtypeStruct((8, 128), jnp.float32),
        in_specs=[pl.BlockSpec(memory_space=pltpu.VMEM)],
        out_specs=pl.BlockSpec(memory_space=pltpu.VMEM),
        compiler_params=pltpu.CompilerParams(vmem_limit_bytes=1024 * 1024),
        cost_estimate=pl.CostEstimate(flops=int(STEP_FLOPS), bytes_accessed=4096, transcendentals=0),
    )(mark)
    return mark, waited


def shards(activations, out_grads, projector, first_moment, second_moment, prev_norm):
    me = lax.axis_index("row")
    at, yt = prologue(activations, projector)
    at_all = lax.all_gather(at, "col")

    got = {hop: {} for hop in range(-3, 5)}
    for t in range(TS):
        got[0][t] = out_grads[t * TK : (t + 1) * TK]
    sent = [(hop, t) for hop in (1, 2, 3) for t in range(TS)] + [(4, t) for t in range(TS // 2)]

    def key(entry, way):
        hop, t = entry
        if hop == 4:
            return 4, t if way == 1 else t + TS // 2
        return way * hop, t

    def listed(*hops):
        ids = jnp.stack([lax.rem(me - hop + ROWS, ROWS) for hop in hops]).astype(jnp.int32)
        return ids, [got[hop][t] for hop in hops for t in range(TS)]

    blocks = yt.reshape(ROWS, 2, RB // 2, CB)

    def own_ranks(way, hop):
        block = lax.rem(me - way * (1 + hop) + 2 * ROWS, ROWS)
        return lax.dynamic_index_in_dim(blocks[:, 0 if way == 1 else 1], block, keepdims=False)

    moving = {way: shift(own_ranks(way, 0), way) for way in (1, -1)}

    mark = jnp.zeros((8, 128), jnp.float32)
    for number, entry in enumerate(sent):
        if number >= 2:
            keys = [key(sent[number - 2], way) for way in (1, -1)]
            waited = [got[hop][t] for hop, t in keys]
            if number == 10:
                (w,) = products(*listed(0, 1, -1), (at_all,), (False,))
                waited.append(w)
            if number == 12:
                (w,) = products(*listed(2, -2), (at_all,), (False,), (w,))
                waited.append(w)
            mark, waited = step_mark(mark, waited)
            for (hop, t), value in zip(keys, waited):
                got[hop][t] = value
            if len(waited) > 2:
                w = waited[2]
            if number <= 7:
                for way in (1, -1):
                    part, (mark,) = gated(moving[way], [mark])
                    part = part + own_ranks(way, number - 1)
                    moving[way] = shift(part, way)
                    part, (mark,) = gated(part, [mark])
            if number == 8:
                ends = [gated(moving[way], [mark])[0] + own_ranks(way, 7) for way in (1, -1)]
                part = jnp.concatenate(ends, axis=0)
                high = lax.optimization_barrier(part.astype(jnp.bfloat16))
                low = (part - high.astype(jnp.float32)).astype(jnp.bfloat16)
                yt_all = lax.all_gather(jnp.concatenate([high, low], axis=0), "col")
        for way in (1, -1):
            hop, t = key(entry, way)
            before = (3 * way if hop == 4 else hop - way)
            src = got[before][t]
            if number >= 2:
                src, (mark,) = gated(src, [mark])
            got[hop][t] = shift(src, way)

    (w,) = products(*listed(3, -3), (at_all,), (False,), (w,), (mark,))
    (p,) = products(*listed(0, 1, -1, 2, -2, 3, -3), (yt_all,), (True,))
    w, p = products(*listed(4), (at_all, yt_all), (False, True), (w, p))

    ways = []
    for way in (1, -1):
        one = shift(p, way)
        two = shift(one, way)
        three = shift(two, way)
        half = three[: RB // 2] if way == 1 else three[RB // 2 :]
        ways.append((one, two, three, shift(half, way)))
    up, down = ways
    pieces = (p, *up[:3], *down[:3], up[3], down[3])

    where = me.reshape(1).astype(jnp.int32)
    scaled, low_rank, n1, n2, total = columns(where, w, pieces, projector, first_moment, second_moment)
    over_row = jnp.sum(lax.all_to_all(total, "row", 0, 0, tiled=True), axis=0)
    sums = lax.all_to_all(jnp.broadcast_to(over_row[None], (COLS, 8, 128)), "col", 0, 0, tiled=True)
    return (final(prev_norm, sums, scaled, low_rank), n1, n2)


def solution(mesh):
    return jax.shard_map(
        shards,
        mesh=mesh,
        in_specs=(
            P("col", "row"),
            P("row", "col"),
            P("row", None),
            P(None, "col"),
            P(None, "col"),
            P(),
        ),
        out_specs=(P("row", "col"), P(None, "col"), P(None, "col")),
        check_vma=False,
    )
```

```python
import functools

import jax
import jax.numpy as jnp
from jax import lax
from jax.experimental import pallas as pl
from jax.experimental.pallas import tpu as pltpu
from jax.sharding import PartitionSpec as P

D = 6144
FF = 24576
RANK = 512

beta_one = 0.9
beta_two = 0.95
corr_one = 1.0 - 0.9**10
corr_two = 1.0 - 0.95**10
growth = 1.01

ROWS = 8
COLS = 32
DR = D // ROWS
FC = FF // COLS
TK = 256
TS = 4
CB = 256
CW = 256
RB = RANK // ROWS
SB = TS * TK // CB
VMEM_LIMIT = 24 * 1024 * 1024
VMEM_MOST = 58 * 1024 * 1024
STEP_FLOPS = 8.0e9


def whole(shape):
    return pl.BlockSpec(shape, lambda *_: (0,) * len(shape))


def prologue_kernel(act_ref, proj_ref, at_ref, yt_ref):
    at = act_ref[...].T
    at_ref[...] = at
    yt_ref[...] = lax.dot_general(
        proj_ref[...], at, (((0,), (0,)), ((), ())), preferred_element_type=jnp.float32
    )


def prologue(activations, projector):
    return pl.pallas_call(
        prologue_kernel,
        out_shape=[
            jax.ShapeDtypeStruct((DR, CB), jnp.bfloat16),
            jax.ShapeDtypeStruct((RANK, CB), jnp.float32),
        ],
        compiler_params=pltpu.CompilerParams(vmem_limit_bytes=VMEM_MOST),
    )(activations, projector)


def product_kernel(count, ranked, resumed, waited, ids, *refs):
    refs = list(refs)
    lefts = [refs.pop(0) for _ in ranked]
    starts = [refs.pop(0) for _ in ranked] if resumed else None
    pieces, refs = refs[: TS * count], refs[TS * count + waited :]
    outs, held, (right_held, sems, right_sems) = refs[: len(ranked)], refs[len(ranked) : -3], refs[-3:]

    def right_copy(index, t):
        return pltpu.make_async_copy(
            pieces[TS * index + t], right_held.at[index, pl.ds(t * TK, TK)], right_sems.at[index, t]
        )

    def copy(which, index):
        rows = pl.ds(ids[index] * SB, SB)
        return pltpu.make_async_copy(lefts[which].at[rows], held[which].at[index], sems.at[which, index])

    for index in range(count):
        for t in range(TS):
            right_copy(index, t).start()
        for which in range(len(ranked)):
            copy(which, index).start()
    for index in range(count):
        for t in range(TS):
            right_copy(index, t).wait()
        right = right_held[index]
        for which, is_ranked in enumerate(ranked):
            copy(which, index).wait()
            left = held[which]
            wide = jnp.concatenate([left[index, block] for block in range(SB)], axis=1)
            got = jnp.dot(wide, right, preferred_element_type=jnp.float32)
            part = got[:RB] + got[RB:] if is_ranked else got
            out = outs[which]
            if index > 0:
                out[...] += part
            else:
                out[...] = starts[which][...] + part if resumed else part


def products(ids, pieces, lefts, ranked, starts=(), waited=(), limit=52 * 2**20):
    count = len(pieces) // TS
    resumed = len(starts) > 0
    width = pieces[0].shape[1]
    specs = [pl.BlockSpec(memory_space=pltpu.SMEM)]
    specs += [pl.BlockSpec(memory_space=pltpu.HBM)] * len(lefts)
    specs += [pl.BlockSpec(memory_space=pltpu.VMEM)] * len(starts)
    specs += [pl.BlockSpec(memory_space=pltpu.HBM)] * (len(pieces) + len(waited))
    heights, rows = [], 0
    for left, is_ranked in zip(lefts, ranked):
        rows += left.shape[1]
        heights.append(RB if is_ranked else left.shape[1])
    return pl.pallas_call(
        functools.partial(product_kernel, count, ranked, resumed, len(waited)),
        out_shape=[jax.ShapeDtypeStruct((h, width), jnp.float32) for h in heights],
        in_specs=specs,
        out_specs=[pl.BlockSpec(memory_space=pltpu.VMEM)] * len(heights),
        scratch_shapes=[
            *[pltpu.VMEM((count, SB) + left.shape[1:], jnp.bfloat16) for left in lefts],
            pltpu.VMEM((count, TS * TK, width), jnp.bfloat16),
            pltpu.SemaphoreType.DMA((len(lefts), count)),
            pltpu.SemaphoreType.DMA((count, TS)),
        ],
        compiler_params=pltpu.CompilerParams(vmem_limit_bytes=limit),
        cost_estimate=pl.CostEstimate(
            flops=2 * rows * TS * TK * width * count,
            bytes_accessed=count * TS * TK * (rows + width) * 2 + rows * width * 4,
            transcendentals=0,
        ),
    )(ids, *lefts, *starts, *pieces, *waited)


def halves(values):
    high = values.astype(jnp.bfloat16)
    return high, (values - high.astype(jnp.float32)).astype(jnp.bfloat16)


def times(left, values):
    high, low = halves(values)
    return jnp.dot(left, high, preferred_element_type=jnp.float32) + jnp.dot(
        left, low, preferred_element_type=jnp.float32
    )


def column_kernel(where, w_ref, *refs):
    refs = list(refs)
    pieces = [refs.pop(0) for _ in range(ROWS + 1)]
    proj_ref, m1_ref, m2_ref, scaled_ref, low_ref, n1_ref, n2_ref, sum_out, projected_ref = refs
    me = where[0]
    for piece, hop in zip(pieces, (0, 1, 2, 3, -1, -2, -3)):
        block = lax.rem(me - hop + ROWS, ROWS)
        projected_ref[pl.ds(pl.multiple_of(block * RB, RB), RB), :] = piece[...]
    block = lax.rem(me + 4, ROWS)
    opposite = jnp.concatenate([pieces[-2][...], pieces[-1][...]], axis=0)
    projected_ref[pl.ds(pl.multiple_of(block * RB, RB), RB), :] = opposite
    projected = projected_ref[...]
    new_first = beta_one * m1_ref[...] + (1.0 - beta_one) * projected
    square = projected * projected
    new_second = beta_two * m2_ref[...] + (1.0 - beta_two) * square
    n1_ref[...] = new_first
    n2_ref[...] = new_second
    adam_dir = new_first * (1.0 / corr_one) / (jnp.sqrt(new_second * (1.0 / corr_two)) + 1e-08)
    col_scale = jnp.sqrt(jnp.sum(adam_dir * adam_dir, axis=0, keepdims=True)) / jnp.sqrt(
        jnp.sum(square, axis=0, keepdims=True) + 1e-06
    )
    left = proj_ref[...]
    residual = w_ref[...] - times(left, projected)
    resid_sq = jnp.sum(residual * residual, axis=0, keepdims=True)
    scaled_ref[...] = col_scale * residual
    low_ref[...] = times(left, adam_dir)
    total = jnp.sum(col_scale * col_scale * resid_sq, axis=1, keepdims=True)
    total = jnp.broadcast_to(total[None], sum_out.shape)

    @pl.when(pl.program_id(0) == 0)
    def _():
        sum_out[...] = total

    @pl.when(pl.program_id(0) > 0)
    def _():
        sum_out[...] += total


def columns(where, w, pieces, projector, first, second):
    def block(rows):
        return pl.BlockSpec((rows, CW), lambda i, ids: (0, i))

    args = [w, *pieces, projector, first, second]
    specs = [block(w.shape[0])] + [block(x.shape[0]) for x in pieces]
    specs += [whole(projector.shape), block(RANK), block(RANK)]
    return pl.pallas_call(
        column_kernel,
        out_shape=[
            jax.ShapeDtypeStruct((DR, FC), jnp.float32),
            jax.ShapeDtypeStruct((DR, FC), jnp.float32),
            jax.ShapeDtypeStruct((RANK, FC), jnp.float32),
            jax.ShapeDtypeStruct((RANK, FC), jnp.float32),
            jax.ShapeDtypeStruct((ROWS, 8, 128), jnp.float32),
        ],
        grid_spec=pltpu.PrefetchScalarGridSpec(
            num_scalar_prefetch=1,
            grid=(FC // CW,),
            in_specs=specs,
            out_specs=[block(DR), block(DR), block(RANK), block(RANK), whole((ROWS, 8, 128))],
            scratch_shapes=[pltpu.VMEM((RANK, CW), jnp.float32)],
        ),
        compiler_params=pltpu.CompilerParams(vmem_limit_bytes=VMEM_MOST),
        cost_estimate=pl.CostEstimate(
            flops=8 * DR * RANK * FC, bytes_accessed=16 * RANK * FC + 12 * DR * FC, transcendentals=0
        ),
    )(where, *args)


def final_kernel(prev_ref, sums_ref, scaled_ref, low_ref, out_ref):
    total = jnp.sum(sums_ref[...], axis=0)[:1, :1]
    clip = growth * prev_ref[0] / jnp.sqrt(total / (D * FF) + 1e-06)
    out_ref[...] = low_ref[...] + clip * scaled_ref[...]


def final(prev_norm, sums, scaled, low):
    tile = pl.BlockSpec((128, FC), lambda i: (i, 0))
    return pl.pallas_call(
        final_kernel,
        out_shape=jax.ShapeDtypeStruct((DR, FC), jnp.float32),
        grid=(DR // 128,),
        in_specs=[pl.BlockSpec(memory_space=pltpu.SMEM), whole(sums.shape), tile, tile],
        out_specs=tile,
        compiler_params=pltpu.CompilerParams(vmem_limit_bytes=VMEM_MOST),
    )(prev_norm, sums, scaled, low)


def shift(values, by):
    return lax.ppermute(values, "row", [(i, (i + by) % ROWS) for i in range(ROWS)])


def gated(values, after):
    values, *after = lax.optimization_barrier((values, *after))
    return values, after


def mark_kernel(mark_ref, out_ref):
    out_ref[...] = mark_ref[...]


def step_mark(mark, waited):
    mark, waited = gated(mark, waited)
    mark = pl.pallas_call(
        mark_kernel,
        out_shape=jax.ShapeDtypeStruct((8, 128), jnp.float32),
        in_specs=[pl.BlockSpec(memory_space=pltpu.VMEM)],
        out_specs=pl.BlockSpec(memory_space=pltpu.VMEM),
        compiler_params=pltpu.CompilerParams(vmem_limit_bytes=1024 * 1024),
        cost_estimate=pl.CostEstimate(flops=int(STEP_FLOPS), bytes_accessed=4096, transcendentals=0),
    )(mark)
    return mark, waited


def shards(activations, out_grads, projector, first_moment, second_moment, prev_norm):
    me = lax.axis_index("row")
    at, yt = prologue(activations, projector)
    at_all = lax.all_gather(at, "col")

    got = {hop: {} for hop in range(-3, 5)}
    for t in range(TS):
        got[0][t] = out_grads[t * TK : (t + 1) * TK]
    sent = [(hop, t) for hop in (1, 2, 3) for t in range(TS)] + [(4, t) for t in range(TS // 2)]

    def key(entry, way):
        hop, t = entry
        if hop == 4:
            return 4, t if way == 1 else t + TS // 2
        return way * hop, t

    def listed(*hops):
        ids = jnp.stack([lax.rem(me - hop + ROWS, ROWS) for hop in hops]).astype(jnp.int32)
        return ids, [got[hop][t] for hop in hops for t in range(TS)]

    blocks = yt.reshape(ROWS, 2, RB // 2, CB)

    def own_ranks(way, hop):
        block = lax.rem(me - way * (1 + hop) + 2 * ROWS, ROWS)
        return lax.dynamic_index_in_dim(blocks[:, 0 if way == 1 else 1], block, keepdims=False)

    moving = {}
    for way in (1, -1):
        part = shift(own_ranks(way, 0), way) + own_ranks(way, 1)
        moving[way] = shift(part, way)
        for t in range(TS):
            got[0][t], (part,) = gated(got[0][t], [part])
        mark = mark + part[:8, :128] if way == -1 else part[:8, :128]

    for number, entry in enumerate(sent):
        if number >= 2:
            keys = [key(sent[number - 2], way) for way in (1, -1)]
            waited = [got[hop][t] for hop, t in keys]
            if 8 <= number <= 12:
                before = () if number == 8 else (w,)
                (w,) = products(*listed((0, 1, -1, 2, -2)[number - 8]), (at_all,), (False,), before)
                waited.append(w)
            mark, waited = step_mark(mark, waited)
            for (hop, t), value in zip(keys, waited):
                got[hop][t] = value
            if 8 <= number <= 12:
                w = waited[2]
            if number <= 6:
                for way in (1, -1):
                    part, (mark,) = gated(moving[way], [mark])
                    part = part + own_ranks(way, number)
                    moving[way] = shift(part, way)
                    part, (mark,) = gated(part, [mark])
            if number == 7:
                ends = []
                for way in (1, -1):
                    part, (mark,) = gated(moving[way], [mark])
                    ends.append(part + own_ranks(way, 7))
                part = jnp.concatenate(ends, axis=0)
                high = lax.optimization_barrier(part.astype(jnp.bfloat16))
                low = (part - high.astype(jnp.float32)).astype(jnp.bfloat16)
                both, (mark,) = gated(jnp.concatenate([high, low], axis=0), [mark])
                yt_all = lax.all_gather(both, "col")
        for way in (1, -1):
            hop, t = key(entry, way)
            src = got[3 * way if hop == 4 else hop - way][t]
            if number >= 2:
                src, (mark,) = gated(src, [mark])
            got[hop][t] = shift(src, way)

    (p,) = products(*listed(0, 1, -1, 2, -2, 3, -3), (yt_all,), (True,), (), (mark,))
    (p,) = products(*listed(4), (yt_all,), (True,), (p,))

    ways, moved = {1: [], -1: []}, {1: p, -1: p}
    for hop, source in ((1, 3), (2, -3), (3, 4), (4, None)):
        if source is not None:
            w, (moved[1], moved[-1]) = gated(w, [moved[1], moved[-1]])
        if hop == 4:
            moved = {1: moved[1][: RB // 2], -1: moved[-1][RB // 2 :]}
        for way in (1, -1):
            moved[way] = shift(moved[way], way)
            ways[way].append(moved[way])
        if source is not None:
            (w,) = products(*listed(source), (at_all,), (False,), (w,), limit=VMEM_LIMIT)
            for way in (1, -1):
                moved[way], (w,) = gated(moved[way], [w])
                ways[way][-1] = moved[way]
    up, down = ways[1], ways[-1]
    pieces = (p, *up[:3], *down[:3], up[3], down[3])

    where = me.reshape(1).astype(jnp.int32)
    scaled, low_rank, n1, n2, total = columns(where, w, pieces, projector, first_moment, second_moment)
    over_row = jnp.sum(lax.all_to_all(total, "row", 0, 0, tiled=True), axis=0)
    sums = lax.all_to_all(jnp.broadcast_to(over_row[None], (COLS, 8, 128)), "col", 0, 0, tiled=True)
    return (final(prev_norm, sums, scaled, low_rank), n1, n2)


def solution(mesh):
    return jax.shard_map(
        shards,
        mesh=mesh,
        in_specs=(
            P("col", "row"),
            P("row", "col"),
            P("row", None),
            P(None, "col"),
            P(None, "col"),
            P(),
        ),
        out_specs=(P("row", "col"), P(None, "col"), P(None, "col")),
        check_vma=False,
    )
```

```python
import functools

import jax
import jax.numpy as jnp
from jax import lax
from jax.experimental import pallas as pl
from jax.experimental.pallas import tpu as pltpu
from jax.sharding import PartitionSpec as P

D = 6144
FF = 24576
RANK = 512

beta_one = 0.9
beta_two = 0.95
corr_one = 1.0 - 0.9**10
corr_two = 1.0 - 0.95**10
growth = 1.01

ROWS = 8
COLS = 32
DR = D // ROWS
FC = FF // COLS
TK = 256
TS = 4
CB = 256
CW = 256
RB = RANK // ROWS
SB = TS * TK // CB
VMEM_LIMIT = 24 * 1024 * 1024
VMEM_MOST = 58 * 1024 * 1024
STEP_FLOPS = 8.0e9


def whole(shape):
    return pl.BlockSpec(shape, lambda *_: (0,) * len(shape))


def prologue_kernel(act_ref, proj_ref, at_ref, yt_ref):
    at = act_ref[...].T
    at_ref[...] = at
    yt_ref[...] = lax.dot_general(
        proj_ref[...], at, (((0,), (0,)), ((), ())), preferred_element_type=jnp.float32
    )


def prologue(activations, projector):
    return pl.pallas_call(
        prologue_kernel,
        out_shape=[
            jax.ShapeDtypeStruct((DR, CB), jnp.bfloat16),
            jax.ShapeDtypeStruct((RANK, CB), jnp.float32),
        ],
        compiler_params=pltpu.CompilerParams(vmem_limit_bytes=VMEM_MOST),
    )(activations, projector)


def product_kernel(count, ranked, resumed, waited, ids, *refs):
    refs = list(refs)
    lefts = [refs.pop(0) for _ in ranked]
    starts = [refs.pop(0) for _ in ranked] if resumed else None
    pieces, refs = refs[: TS * count], refs[TS * count + waited :]
    outs, held, (right_held, sems, right_sems) = refs[: len(ranked)], refs[len(ranked) : -3], refs[-3:]

    def right_copy(index, t):
        return pltpu.make_async_copy(
            pieces[TS * index + t], right_held.at[index, pl.ds(t * TK, TK)], right_sems.at[index, t]
        )

    def copy(which, index):
        rows = pl.ds(ids[index] * SB, SB)
        return pltpu.make_async_copy(lefts[which].at[rows], held[which].at[index], sems.at[which, index])

    for index in range(count):
        for t in range(TS):
            right_copy(index, t).start()
        for which in range(len(ranked)):
            copy(which, index).start()
    for index in range(count):
        for t in range(TS):
            right_copy(index, t).wait()
        right = right_held[index]
        for which, is_ranked in enumerate(ranked):
            copy(which, index).wait()
            left = held[which]
            wide = jnp.concatenate([left[index, block] for block in range(SB)], axis=1)
            got = jnp.dot(wide, right, preferred_element_type=jnp.float32)
            part = got[:RB] + got[RB:] if is_ranked else got
            out = outs[which]
            if index > 0:
                out[...] += part
            else:
                out[...] = starts[which][...] + part if resumed else part


def products(ids, pieces, lefts, ranked, starts=(), waited=(), limit=52 * 2**20):
    count = len(pieces) // TS
    resumed = len(starts) > 0
    width = pieces[0].shape[1]
    specs = [pl.BlockSpec(memory_space=pltpu.SMEM)]
    specs += [pl.BlockSpec(memory_space=pltpu.HBM)] * len(lefts)
    specs += [pl.BlockSpec(memory_space=pltpu.VMEM)] * len(starts)
    specs += [pl.BlockSpec(memory_space=pltpu.HBM)] * (len(pieces) + len(waited))
    heights, rows = [], 0
    for left, is_ranked in zip(lefts, ranked):
        rows += left.shape[1]
        heights.append(RB if is_ranked else left.shape[1])
    return pl.pallas_call(
        functools.partial(product_kernel, count, ranked, resumed, len(waited)),
        out_shape=[jax.ShapeDtypeStruct((h, width), jnp.float32) for h in heights],
        in_specs=specs,
        out_specs=[pl.BlockSpec(memory_space=pltpu.VMEM)] * len(heights),
        scratch_shapes=[
            *[pltpu.VMEM((count, SB) + left.shape[1:], jnp.bfloat16) for left in lefts],
            pltpu.VMEM((count, TS * TK, width), jnp.bfloat16),
            pltpu.SemaphoreType.DMA((len(lefts), count)),
            pltpu.SemaphoreType.DMA((count, TS)),
        ],
        compiler_params=pltpu.CompilerParams(vmem_limit_bytes=limit),
        cost_estimate=pl.CostEstimate(
            flops=2 * rows * TS * TK * width * count,
            bytes_accessed=count * TS * TK * (rows + width) * 2 + rows * width * 4,
            transcendentals=0,
        ),
    )(ids, *lefts, *starts, *pieces, *waited)


def halves(values):
    high = values.astype(jnp.bfloat16)
    return high, (values - high.astype(jnp.float32)).astype(jnp.bfloat16)


def times(left, values):
    high, low = halves(values)
    return jnp.dot(left, high, preferred_element_type=jnp.float32) + jnp.dot(
        left, low, preferred_element_type=jnp.float32
    )


def column_kernel(where, w_ref, *refs):
    refs = list(refs)
    pieces = [refs.pop(0) for _ in range(ROWS + 1)]
    proj_ref, m1_ref, m2_ref, scaled_ref, low_ref, n1_ref, n2_ref, sum_out, projected_ref = refs
    me = where[0]
    for piece, hop in zip(pieces, (0, 1, 2, 3, -1, -2, -3)):
        block = lax.rem(me - hop + ROWS, ROWS)
        projected_ref[pl.ds(pl.multiple_of(block * RB, RB), RB), :] = piece[...]
    block = lax.rem(me + 4, ROWS)
    opposite = jnp.concatenate([pieces[-2][...], pieces[-1][...]], axis=0)
    projected_ref[pl.ds(pl.multiple_of(block * RB, RB), RB), :] = opposite
    projected = projected_ref[...]
    new_first = beta_one * m1_ref[...] + (1.0 - beta_one) * projected
    square = projected * projected
    new_second = beta_two * m2_ref[...] + (1.0 - beta_two) * square
    n1_ref[...] = new_first
    n2_ref[...] = new_second
    adam_dir = new_first * (1.0 / corr_one) / (jnp.sqrt(new_second * (1.0 / corr_two)) + 1e-08)
    col_scale = jnp.sqrt(jnp.sum(adam_dir * adam_dir, axis=0, keepdims=True)) / jnp.sqrt(
        jnp.sum(square, axis=0, keepdims=True) + 1e-06
    )
    left = proj_ref[...]
    residual = w_ref[...] - times(left, projected)
    resid_sq = jnp.sum(residual * residual, axis=0, keepdims=True)
    scaled_ref[...] = col_scale * residual
    low_ref[...] = times(left, adam_dir)
    total = jnp.sum(col_scale * col_scale * resid_sq, axis=1, keepdims=True)
    total = jnp.broadcast_to(total[None], sum_out.shape)

    @pl.when(pl.program_id(0) == 0)
    def _():
        sum_out[...] = total

    @pl.when(pl.program_id(0) > 0)
    def _():
        sum_out[...] += total


def columns(where, w, pieces, projector, first, second):
    def block(rows):
        return pl.BlockSpec((rows, CW), lambda i, ids: (0, i))

    args = [w, *pieces, projector, first, second]
    specs = [block(w.shape[0])] + [block(x.shape[0]) for x in pieces]
    specs += [whole(projector.shape), block(RANK), block(RANK)]
    return pl.pallas_call(
        column_kernel,
        out_shape=[
            jax.ShapeDtypeStruct((DR, FC), jnp.float32),
            jax.ShapeDtypeStruct((DR, FC), jnp.float32),
            jax.ShapeDtypeStruct((RANK, FC), jnp.float32),
            jax.ShapeDtypeStruct((RANK, FC), jnp.float32),
            jax.ShapeDtypeStruct((ROWS, 8, 128), jnp.float32),
        ],
        grid_spec=pltpu.PrefetchScalarGridSpec(
            num_scalar_prefetch=1,
            grid=(FC // CW,),
            in_specs=specs,
            out_specs=[block(DR), block(DR), block(RANK), block(RANK), whole((ROWS, 8, 128))],
            scratch_shapes=[pltpu.VMEM((RANK, CW), jnp.float32)],
        ),
        compiler_params=pltpu.CompilerParams(vmem_limit_bytes=VMEM_MOST),
        cost_estimate=pl.CostEstimate(
            flops=8 * DR * RANK * FC, bytes_accessed=16 * RANK * FC + 12 * DR * FC, transcendentals=0
        ),
    )(where, *args)


def final_kernel(prev_ref, sums_ref, scaled_ref, low_ref, out_ref):
    total = jnp.sum(sums_ref[...], axis=0)[:1, :1]
    clip = growth * prev_ref[0] / jnp.sqrt(total / (D * FF) + 1e-06)
    out_ref[...] = low_ref[...] + clip * scaled_ref[...]


def final(prev_norm, sums, scaled, low):
    tile = pl.BlockSpec((128, FC), lambda i: (i, 0))
    return pl.pallas_call(
        final_kernel,
        out_shape=jax.ShapeDtypeStruct((DR, FC), jnp.float32),
        grid=(DR // 128,),
        in_specs=[pl.BlockSpec(memory_space=pltpu.SMEM), whole(sums.shape), tile, tile],
        out_specs=tile,
        compiler_params=pltpu.CompilerParams(vmem_limit_bytes=VMEM_MOST),
    )(prev_norm, sums, scaled, low)


def shift(values, by):
    return lax.ppermute(values, "row", [(i, (i + by) % ROWS) for i in range(ROWS)])


def gated(values, after):
    values, *after = lax.optimization_barrier((values, *after))
    return values, after


def mark_kernel(mark_ref, out_ref):
    out_ref[...] = mark_ref[...]


def step_mark(mark, waited):
    mark, waited = gated(mark, waited)
    mark = pl.pallas_call(
        mark_kernel,
        out_shape=jax.ShapeDtypeStruct((8, 128), jnp.float32),
        in_specs=[pl.BlockSpec(memory_space=pltpu.VMEM)],
        out_specs=pl.BlockSpec(memory_space=pltpu.VMEM),
        compiler_params=pltpu.CompilerParams(vmem_limit_bytes=1024 * 1024),
        cost_estimate=pl.CostEstimate(flops=int(STEP_FLOPS), bytes_accessed=4096, transcendentals=0),
    )(mark)
    return mark, waited


def shards(activations, out_grads, projector, first_moment, second_moment, prev_norm):
    me = lax.axis_index("row")
    at, yt = prologue(activations, projector)
    at_all = lax.all_gather(at, "col")

    got = {hop: {} for hop in range(-3, 5)}
    for t in range(TS):
        got[0][t] = out_grads[t * TK : (t + 1) * TK]
    sent = [(hop, t) for hop in (1, 2, 3) for t in range(TS)] + [(4, t) for t in range(TS // 2)]

    def key(entry, way):
        hop, t = entry
        if hop == 4:
            return 4, t if way == 1 else t + TS // 2
        return way * hop, t

    def listed(*hops):
        ids = jnp.stack([lax.rem(me - hop + ROWS, ROWS) for hop in hops]).astype(jnp.int32)
        return ids, [got[hop][t] for hop in hops for t in range(TS)]

    blocks = yt.reshape(ROWS, 2, RB // 2, CB)

    def own_ranks(way, hop):
        block = lax.rem(me - way * (1 + hop) + 2 * ROWS, ROWS)
        return lax.dynamic_index_in_dim(blocks[:, 0 if way == 1 else 1], block, keepdims=False)

    moving = {}
    for way in (1, -1):
        part = own_ranks(way, 0)
        got[0][0], (part,) = gated(got[0][0], [part])
        part = shift(part, way) + own_ranks(way, 1)
        moving[way] = shift(part, way)
        for t in range(1, TS):
            got[0][t], (part,) = gated(got[0][t], [part])
        mark = mark + part[:8, :128] if way == -1 else part[:8, :128]

    for number, entry in enumerate(sent):
        if number >= 2:
            keys = [key(sent[number - 2], way) for way in (1, -1)]
            waited = [got[hop][t] for hop, t in keys]
            if 8 <= number <= 12:
                before = () if number == 8 else (w,)
                (w,) = products(*listed((0, 1, -1, 2, -2)[number - 8]), (at_all,), (False,), before)
                waited.append(w)
            mark, waited = step_mark(mark, waited)
            for (hop, t), value in zip(keys, waited):
                got[hop][t] = value
            if 8 <= number <= 12:
                w = waited[2]
            if number <= 6:
                for way in (1, -1):
                    part, (mark,) = gated(moving[way], [mark])
                    part = part + own_ranks(way, number)
                    moving[way] = shift(part, way)
                    part, (mark,) = gated(part, [mark])
            if number == 7:
                ends = []
                for way in (1, -1):
                    part, (mark,) = gated(moving[way], [mark])
                    ends.append(part + own_ranks(way, 7))
                part = jnp.concatenate(ends, axis=0)
                high = lax.optimization_barrier(part.astype(jnp.bfloat16))
                low = (part - high.astype(jnp.float32)).astype(jnp.bfloat16)
                both, (mark,) = gated(jnp.concatenate([high, low], axis=0), [mark])
                yt_all = lax.all_gather(both, "col")
        for way in (1, -1):
            hop, t = key(entry, way)
            src = got[3 * way if hop == 4 else hop - way][t]
            if number >= 2:
                src, (mark,) = gated(src, [mark])
            got[hop][t] = shift(src, way)

    (p,) = products(*listed(0, 1, -1, 2, -2, 3, -3), (yt_all,), (True,), (), (mark,))
    (p,) = products(*listed(4), (yt_all,), (True,), (p,))

    ways, moved = {1: [], -1: []}, {1: p, -1: p}
    for hop, source in ((1, 3), (2, -3), (3, 4), (4, None)):
        if source is not None:
            w, (moved[1], moved[-1]) = gated(w, [moved[1], moved[-1]])
        if hop == 4:
            moved = {1: moved[1][: RB // 2], -1: moved[-1][RB // 2 :]}
        for way in (1, -1):
            moved[way] = shift(moved[way], way)
            ways[way].append(moved[way])
        if source is not None:
            (w,) = products(*listed(source), (at_all,), (False,), (w,), limit=VMEM_LIMIT)
            for way in (1, -1):
                moved[way], (w,) = gated(moved[way], [w])
                ways[way][-1] = moved[way]
    up, down = ways[1], ways[-1]
    pieces = (p, *up[:3], *down[:3], up[3], down[3])

    where = me.reshape(1).astype(jnp.int32)
    scaled, low_rank, n1, n2, total = columns(where, w, pieces, projector, first_moment, second_moment)
    over_row = jnp.sum(lax.all_to_all(total, "row", 0, 0, tiled=True), axis=0)
    sums = lax.all_to_all(jnp.broadcast_to(over_row[None], (COLS, 8, 128)), "col", 0, 0, tiled=True)
    return (final(prev_norm, sums, scaled, low_rank), n1, n2)


def solution(mesh):
    return jax.shard_map(
        shards,
        mesh=mesh,
        in_specs=(
            P("col", "row"),
            P("row", "col"),
            P("row", None),
            P(None, "col"),
            P(None, "col"),
            P(),
        ),
        out_specs=(P("row", "col"), P(None, "col"), P(None, "col")),
        check_vma=False,
    )
```
